32 devices in a mesh: row: 4 (over x, core), col: 4 (over z), depth: 2 (over y).
Axes of the slice: x: 2, y: 2, z: 4, core: 2. Of those that a mesh axis runs over, the one named last changes fastest.
Arguments:
- activations: bfloat16 [4096, 4544], P(('depth', 'row'), 'col'), may hold values from -6 to 6
- out_grads: bfloat16 [4096, 12288], P(('depth', 'col'), 'row'), may hold values from -0.125 to 0.125
Outputs:
- weight_grad: float32 [12288, 4544], P(('row', 'depth'), 'col')
The draws below stay inside these ranges and needn't reach their ends.
All inputs are finite; a program needn't handle non-finite values.
Results may differ from the reference program's by a relative error of at most 0.0003.
Values may be sent and summed in bfloat16 or wider, within the bound.
A program may use at most 128 MiB of HBM per device.

```python
import jax
import jax.numpy as jnp
from jax import lax

D = 4544
FFW = 12288
TOKENS = 4096


def raised(result, rng, source, target, parts, factor):
    owner, partner = [(jnp.arange(result.shape[dim]) // (result.shape[dim] // parts)).reshape([-1 if axis == dim else 1 for axis in range(result.ndim)]) for dim in (source, target)]
    chosen = jax.random.permutation(rng, parts)[partner]
    strong = (owner == chosen) | (owner == (partner + parts // 2) % parts)
    return jnp.where(strong, factor * result, result)


def steps_of(stream_key, shape, split, low, top_value):
    gain = 1.0
    for axis_at, shards_of in split:
        heights = jax.random.uniform(jax.random.fold_in(jax.random.fold_in(stream_key, 6), axis_at), (shards_of,), jnp.float32, low / len(split), top_value / len(split))
        gain = gain * jnp.repeat(jnp.exp(heights), shape[axis_at] // shards_of).reshape((-1,) + (1,) * (len(shape) - 1 - axis_at))
    return gain


def scatter_about(stream_key, extent, scale, bound, shards=(), dtype=jnp.bfloat16):
    array = jax.random.normal(stream_key, extent, jnp.float32) * scale
    if len(shards) > 0:
        array = steps_of(stream_key, extent, shards, -0.22, 0.18) * array
    return jnp.clip(array, min=-bound, max=bound).astype(dtype)


def bell_draw_with(key, extent, width, most, shards, heavy, kind=jnp.bfloat16):
    result = width * jax.random.normal(key, extent, jnp.float32)
    if shards:
        result = result * steps_of(key, extent, shards, -0.22, 0.18)
    return jnp.clip(raised(result, jax.random.fold_in(key, 3), *heavy), -most, most).astype(kind)


def setup_inputs(seed: int = 0) -> dict:
    key_of = jax.random.split(jax.random.key(seed), 3)
    activations = scatter_about(key_of[0], (TOKENS, D), 1.0, 6.0, ((0, 8), (1, 4)))
    out_grads = bell_draw_with(key_of[1], (TOKENS, FFW), TOKENS ** -0.5, 0.125, ((0, 8), (1, 4)), (0, 1, 8, 2.0))
    return dict(activations=activations, out_grads=out_grads)


def reference(activations, out_grads):
    return lax.dot_general(out_grads, activations, (((0,), (0,)), ((), ())), preferred_element_type=jnp.float32)
```

```python
import functools

import jax
import jax.numpy as jnp
from jax import lax
from jax.experimental import pallas as pl
from jax.experimental.pallas import tpu as pltpu
from jax.sharding import PartitionSpec as P

MESH = pl.DeviceIdType.MESH
CHUNKS = 2
TILE = 256


def contract(left, right):
    return lax.dot_general(
        left, right, (((0,), (0,)), ((), ())), preferred_element_type=jnp.float32
    )


def gather_acts(activations):
    return lax.all_gather(activations, "row", axis=0, tiled=True)


def body(activations, out_grads):
    whole_acts = gather_acts(activations)
    partial_tile = contract(lax.all_gather(out_grads, "col", axis=0, tiled=True), whole_acts)
    return lax.psum_scatter(partial_tile, "depth", scatter_dimension=0, tiled=True)


def kernel(
    cols, acts_hbm, grads_hbm, out_ref, acts, grads,
    local_sem, acts_recv, acts_send, grads_recv, send_right, send_left, send_y,
):
    r, z, y = lax.axis_index("row"), lax.axis_index("col"), lax.axis_index("depth")
    tokens = acts_hbm.shape[0]
    half = out_ref.shape[0]
    piece = tokens // CHUNKS
    last = cols - 1
    other_y = 1 - y
    sib = r + 1 - 2 * lax.rem(r, 2)
    across = lax.rem(r + 2, 4)
    across_sib = sib + across - r
    to_sib, to_x, to_y = {"row": sib}, {"row": across}, {"depth": other_y}
    to_right, to_left = {"col": jnp.minimum(z + 1, last)}, {"col": jnp.maximum(z - 1, 0)}

    barrier = pltpu.get_barrier_semaphore()
    for partner in (to_sib, to_x, to_y):
        pl.semaphore_signal(barrier, inc=1, device_id=partner, device_id_type=MESH)

    @pl.when(z < last)
    def _():
        pl.semaphore_signal(barrier, inc=1, device_id=to_right, device_id_type=MESH)

    @pl.when(z > 0)
    def _():
        pl.semaphore_signal(barrier, inc=1, device_id=to_left, device_id_type=MESH)

    pl.semaphore_wait(barrier, 3 + (z < last).astype(jnp.int32) + (z > 0).astype(jnp.int32))

    def rows(c):
        return pl.ds(pl.multiple_of(c * piece, piece), piece)

    mine = pl.ds(pl.multiple_of(y * half, half), half)
    theirs = pl.ds(pl.multiple_of(other_y * half, half), half)

    def remote(src, dst, send, recv, device):
        return pltpu.make_async_remote_copy(
            src_ref=src, dst_ref=dst, send_sem=send, recv_sem=recv,
            device_id=device, device_id_type=MESH,
        )

    def swap(c):
        return remote(
            grads_hbm.at[rows(c), theirs], grads.at[y, z, rows(c)],
            send_y.at[c], grads_recv.at[y, z, c], to_y,
        )

    def own_right(c):
        return remote(
            grads_hbm.at[rows(c), mine], grads.at[y, z, rows(c)],
            send_right.at[y, z, c], grads_recv.at[y, z, c], to_right,
        )

    def own_left(c):
        return remote(
            grads_hbm.at[rows(c), mine], grads.at[y, z, rows(c)],
            send_left.at[y, z, c], grads_recv.at[y, z, c], to_left,
        )

    def on_right(yy, zz, c):
        block = grads.at[yy, zz, rows(c)]
        return remote(block, block, send_right.at[yy, zz, c], grads_recv.at[yy, zz, c], to_right)

    def on_left(yy, zz, c):
        block = grads.at[yy, zz, rows(c)]
        return remote(block, block, send_left.at[yy, zz, c], grads_recv.at[yy, zz, c], to_left)

    def arrived(yy, zz, c):
        block = grads.at[yy, zz, rows(c)]
        pltpu.make_async_copy(block, block, grads_recv.at[yy, zz, c]).wait()

    def acts_copy(src, yy, rr, which, device):
        return remote(src, acts.at[yy, rr], acts_send.at[which], acts_recv.at[yy, rr], device)

    def acts_on(yy, rr, which, device):
        return acts_copy(acts.at[yy, rr], yy, rr, which, device)

    def acts_arrived(yy, rr):
        pltpu.make_async_copy(acts.at[yy, rr], acts.at[yy, rr], acts_recv.at[yy, rr]).wait()

    for c in range(CHUNKS):
        swap(c).start()

        @pl.when(z < last)
        def _():
            own_right(c).start()

        @pl.when(z > 0)
        def _():
            own_left(c).start()

    own_to_x = acts_copy(acts_hbm, y, r, 0, to_x)
    own_to_sib = acts_copy(acts_hbm, y, r, 1, to_sib)
    own_to_y = acts_copy(acts_hbm, y, r, 2, to_y)
    own_to_x.start()
    own_to_sib.start()
    keep_acts = pltpu.make_async_copy(acts_hbm, acts.at[y, r], local_sem.at[0])
    keep_grads = pltpu.make_async_copy(grads_hbm.at[:, mine], grads.at[y, z], local_sem.at[1])
    keep_acts.start()
    keep_grads.start()
    out_ref[...] = jnp.zeros_like(out_ref)

    for c in range(CHUNKS):
        arrived(other_y, z, c)

        @pl.when(z < last)
        def _():
            on_right(other_y, z, c).start()

        @pl.when(z > 0)
        def _():
            on_left(other_y, z, c).start()

    own_to_y.start()
    acts_arrived(y, across)
    x_to_sib = acts_on(y, across, 3, to_sib)
    x_to_sib.start()

    def take(step, yy, c):
        from_left = z - step
        from_right = z + step

        @pl.when(from_left >= 0)
        def _():
            arrived(yy, from_left, c)

            @pl.when(z < last)
            def _():
                on_right(yy, from_left, c).start()

        @pl.when(from_right <= last)
        def _():
            arrived(yy, from_right, c)

            @pl.when(z > 0)
            def _():
                on_left(yy, from_right, c).start()

    def multiply(yy, zz, c):
        tile = TILE if half % TILE == 0 else 128

        @pl.loop(0, half // tile)
        def _(i):
            at = pl.ds(pl.multiple_of(i * tile, tile), tile)
            out_ref[at, :] += contract(grads[yy, zz, rows(c), at], acts[yy, zz, rows(c), :])

    def multiply_both(step, yy, c):
        @pl.when(z - step >= 0)
        def _():
            multiply(yy, z - step, c)

        @pl.when(z + step <= last)
        def _():
            multiply(yy, z + step, c)

    acts_arrived(other_y, r)
    diagonal = acts_on(other_y, r, 4, to_x)
    diagonal.start()
    y_to_sib = acts_on(other_y, r, 5, to_sib)
    y_to_sib.start()
    for c in range(CHUNKS):
        take(1, y, c)
    acts_arrived(other_y, across)
    diagonal_to_sib = acts_on(other_y, across, 6, to_sib)
    diagonal_to_sib.start()
    for c in range(CHUNKS):
        take(1, other_y, c)

    keep_acts.wait()
    keep_grads.wait()
    acts_arrived(y, sib)
    acts_arrived(y, across_sib)
    acts_arrived(other_y, sib)
    acts_arrived(other_y, across_sib)

    @pl.loop(0, 2 * CHUNKS)
    def _(i):
        multiply(i // CHUNKS, z, lax.rem(i, CHUNKS))

    @pl.loop(0, 2 * CHUNKS)
    def _(i):
        multiply_both(1, lax.rem(y + i // CHUNKS, 2), lax.rem(i, CHUNKS))

    @pl.loop(0, (cols - 2) * 2 * CHUNKS)
    def _(i):
        step = 2 + i // (2 * CHUNKS)
        yy = lax.rem(y + lax.rem(i, 2 * CHUNKS) // CHUNKS, 2)
        c = lax.rem(i, CHUNKS)
        take(step, yy, c)
        multiply_both(step, yy, c)

    for copy in (own_to_x, own_to_sib, own_to_y, x_to_sib, diagonal, y_to_sib, diagonal_to_sib):
        copy.wait_send()
    for c in range(CHUNKS):
        swap(c).wait_send()

    @pl.loop(0, cols * 2 * CHUNKS)
    def _(i):
        zz = i // (2 * CHUNKS)
        yy = lax.rem(i, 2 * CHUNKS) // CHUNKS
        c = lax.rem(i, CHUNKS)

        @pl.when((z < last) & (zz <= z))
        def _():
            on_right(yy, zz, c).wait_send()

        @pl.when((z > 0) & (zz >= z))
        def _():
            on_left(yy, zz, c).wait_send()


def fused_body(cols, activations, out_grads):
    tokens, width = activations.shape
    half = out_grads.shape[1] // 2
    dma = pltpu.SemaphoreType.DMA
    return pl.pallas_call(
        functools.partial(kernel, cols),
        out_shape=jax.ShapeDtypeStruct((half, width), jnp.float32),
        in_specs=[pl.BlockSpec(memory_space=pl.ANY)] * 2,
        out_specs=pl.BlockSpec(memory_space=pltpu.VMEM),
        scratch_shapes=[
            pltpu.VMEM((2, cols, tokens, width), jnp.bfloat16),
            pltpu.VMEM((2, cols, tokens, half), jnp.bfloat16),
            dma((2,)),
            dma((2, cols)),
            dma((7,)),
            dma((2, cols, CHUNKS)),
            dma((2, cols, CHUNKS)),
            dma((2, cols, CHUNKS)),
            dma((CHUNKS,)),
        ],
        compiler_params=pltpu.CompilerParams(
            collective_id=0, has_side_effects=True, vmem_limit_bytes=56 * 2**20
        ),
        cost_estimate=pl.CostEstimate(
            flops=2 * half * width * tokens * cols * 2,
            bytes_accessed=4 * half * width + 4 * tokens * (width + 2 * half),
            transcendentals=0,
        ),
    )(activations, out_grads)


def solution(mesh):
    in_specs = (P(("depth", "row"), "col"), P(("depth", "col"), "row"))
    out_specs = P(("row", "depth"), "col")
    rows, cols, depth = mesh.shape["row"], mesh.shape["col"], mesh.shape["depth"]

    def local(activations, out_grads):
        tokens, half = out_grads.shape[0], out_grads.shape[1] // depth
        fits = (rows, cols, depth) == (4, 4, 2) and half % 128 == 0 and tokens % 32 == 0
        if fits:
            return fused_body(cols, activations, out_grads)
        return body(activations, out_grads)

    return jax.shard_map(local, mesh=mesh, in_specs=in_specs, out_specs=out_specs, check_vma=False)
```

```python
import jax
import jax.numpy as jnp
from jax import lax
from jax.experimental import pallas as pl
from jax.experimental.pallas import tpu as pltpu
from jax.sharding import PartitionSpec as P

MESH = pl.DeviceIdType.MESH
PIECES = 6
WHOLE = 3


def contract(left, right):
    return lax.dot_general(
        left, right, (((0,), (0,)), ((), ())), preferred_element_type=jnp.float32
    )


def gather_acts(activations):
    return lax.all_gather(activations, "row", axis=0, tiled=True)


def body(activations, out_grads):
    whole_acts = gather_acts(activations)
    partial_tile = contract(lax.all_gather(out_grads, "col", axis=0, tiled=True), whole_acts)
    return lax.psum_scatter(partial_tile, "depth", scatter_dimension=0, tiled=True)


def kernel(
    acts_hbm, grads_hbm, out_hbm, acts, grads, total, sums,
    local_sem, acts_recv, acts_send, grads_recv, send_mate, send_mid, send_y,
    sums_recv, sums_send, out_sem,
):
    r, z, y = lax.axis_index("row"), lax.axis_index("col"), lax.axis_index("depth")
    wide = total.shape[2]
    half = wide * PIECES
    other_y = 1 - y
    sib = r + 1 - 2 * lax.rem(r, 2)
    across = lax.rem(r + 2, 4)
    across_sib = sib + across - r
    mate = z + 1 - 2 * lax.rem(z, 2)
    opposite = 3 - z
    far = 3 - mate
    helper = (z == 1) | (z == 2)
    to_sib, to_x, to_y, to_mate, to_mid = (
        {"row": sib}, {"row": across}, {"depth": other_y}, {"col": mate}, {"col": opposite}
    )

    barrier = pltpu.get_barrier_semaphore()
    for partner in (to_sib, to_x, to_y, to_mate):
        pl.semaphore_signal(barrier, inc=1, device_id=partner, device_id_type=MESH)

    @pl.when(helper)
    def _():
        pl.semaphore_signal(barrier, inc=1, device_id=to_mid, device_id_type=MESH)

    pl.semaphore_wait(barrier, 4 + helper.astype(jnp.int32))

    def remote(src, dst, send, recv, device):
        return pltpu.make_async_remote_copy(
            src_ref=src, dst_ref=dst, send_sem=send, recv_sem=recv,
            device_id=device, device_id_type=MESH,
        )

    def part(yy, p):
        return pl.ds(pl.multiple_of(yy * half + p * wide, wide), wide)

    def swap(p):
        return remote(
            grads_hbm.at[:, part(other_y, p)], grads.at[y, z, p],
            send_y.at[p], grads_recv.at[y, z, p], to_y,
        )

    def own_mate(p):
        return remote(
            grads_hbm.at[:, part(y, p)], grads.at[y, z, p],
            send_mate.at[y, z, p], grads_recv.at[y, z, p], to_mate,
        )

    def own_mid(p):
        return remote(
            grads_hbm.at[:, part(y, p)], grads.at[y, z, p],
            send_mid.at[y, z, p], grads_recv.at[y, z, p], to_mid,
        )

    def on_mate(yy, zz, p):
        block = grads.at[yy, zz, p]
        return remote(block, block, send_mate.at[yy, zz, p], grads_recv.at[yy, zz, p], to_mate)

    def on_mid(yy, zz, p):
        block = grads.at[yy, zz, p]
        return remote(block, block, send_mid.at[yy, zz, p], grads_recv.at[yy, zz, p], to_mid)

    def arrived(yy, zz, p):
        block = grads.at[yy, zz, p]
        pltpu.make_async_copy(block, block, grads_recv.at[yy, zz, p]).wait()

    def acts_copy(src, of, yy, rr, which, device):
        return remote(src, acts.at[of, yy, rr], acts_send.at[of, which], acts_recv.at[of, yy, rr], device)

    def acts_on(of, yy, rr, which, device):
        return acts_copy(acts.at[of, yy, rr], of, yy, rr, which, device)

    def acts_arrived(of, yy, rr):
        block = acts.at[of, yy, rr]
        pltpu.make_async_copy(block, block, acts_recv.at[of, yy, rr]).wait()

    def own_to_x():
        return acts_copy(acts_hbm, 0, y, r, 0, to_x)

    def own_to_sib():
        return acts_copy(acts_hbm, 0, y, r, 1, to_sib)

    def own_to_y():
        return acts_copy(acts_hbm, 0, y, r, 2, to_y)

    def own_to_helper():
        return acts_copy(acts_hbm, 1, y, r, 7, to_mate)

    def x_to_sib(of):
        return acts_on(of, y, across, 3, to_sib)

    def diagonal(of):
        return acts_on(of, other_y, r, 4, to_x)

    def y_to_sib(of):
        return acts_on(of, other_y, r, 5, to_sib)

    def diagonal_to_sib(of):
        return acts_on(of, other_y, across, 6, to_sib)

    def sib_arrived(of):
        for yy in (y, other_y):
            for rr in (sib, across_sib):
                acts_arrived(of, yy, rr)

    def keep_acts():
        return pltpu.make_async_copy(acts_hbm, acts.at[0, y, r], local_sem.at[PIECES])

    def keep_grads(p):
        return pltpu.make_async_copy(grads_hbm.at[:, part(y, p)], grads.at[y, z, p], local_sem.at[p])

    def product(of, yy, zz, p):
        return jnp.dot(acts[of, yy, zz], grads[yy, zz, p], preferred_element_type=jnp.float32)

    def write(p):
        return pltpu.make_async_copy(
            total.at[p], out_hbm.at[:, pl.ds(pl.multiple_of(p * wide, wide), wide)], out_sem.at[p]
        )

    def send_sum(q):
        return remote(sums.at[q], sums.at[q], sums_send.at[q], sums_recv.at[q], to_mate)

    @pl.when(~helper)
    def _():
        own_to_helper().start()

    for p in range(PIECES):
        swap(p).start()
    own_to_x().start()
    own_to_sib().start()

    @pl.when(~helper)
    def _():
        for p in range(PIECES):
            own_mate(p).start()
            arrived(other_y, z, p)
            on_mate(other_y, z, p).start()
        own_to_y().start()
        keep_acts().start()
        for p in range(PIECES):
            keep_grads(p).start()
        acts_arrived(0, y, across)
        x_to_sib(0).start()
        acts_arrived(0, other_y, r)
        diagonal(0).start()
        y_to_sib(0).start()
        acts_arrived(0, other_y, across)
        diagonal_to_sib(0).start()
        keep_acts().wait()
        for p in range(PIECES):
            keep_grads(p).wait()
        sib_arrived(0)

        @pl.loop(0, PIECES)
        def _(p):
            total[p] = product(0, 0, z, p)
            total[p] += product(0, 1, z, p)

        for zz in (mate, far, opposite):
            @pl.loop(0, WHOLE * 2)
            def _(i):
                p, yy = i // 2, lax.rem(y + i, 2)
                arrived(yy, zz, p)
                total[p] += product(0, yy, zz, p)

        for p in range(WHOLE):
            write(p).start()

        @pl.loop(WHOLE, PIECES)
        def _(p):
            q = p - WHOLE
            pltpu.make_async_copy(sums.at[q], sums.at[q], sums_recv.at[q]).wait()
            total[p] += sums[q]
            write(p).start()

        own_to_helper().wait_send()

        @pl.loop(0, PIECES)
        def _(p):
            own_mate(p).wait_send()
            on_mate(other_y, z, p).wait_send()

    @pl.when(helper)
    def _():
        def own_out(p):
            own_mid(p).start()
            if p < WHOLE:
                own_mate(p).start()
            arrived(other_y, z, p)
            on_mid(other_y, z, p).start()
            if p < WHOLE:
                on_mate(other_y, z, p).start()

        def to_the_end(zz, p):
            for yy in (y, other_y):
                arrived(yy, zz, p)
                if p < WHOLE:
                    on_mate(yy, zz, p).start()

        def to_the_middle(p):
            for yy in (y, other_y):
                arrived(yy, mate, p)
                on_mid(yy, mate, p).start()

        def own_product(p):
            total[p] = product(0, 0, 0, p)

            @pl.loop(1, 8)
            def _(i):
                total[p] += product(0, i // 4, lax.rem(i, 4), p)

            write(p).start()

        def sum_for_end(p):
            q = p - WHOLE
            to_the_end(opposite, p)
            to_the_end(far, p)
            sums[q] = product(1, 0, z, p)
            sums[q] += product(1, 1, z, p)

            @pl.loop(0, 4)
            def _(i):
                zz = jnp.where(i < 2, opposite, far)
                sums[q] += product(1, lax.rem(i, 2), zz, p)

            send_sum(q).start()

        for p in range(WHOLE):
            own_out(p)
        acts_arrived(1, y, r)
        e_to_x = acts_on(1, y, r, 0, to_x)
        e_to_sib = acts_on(1, y, r, 1, to_sib)
        e_to_y = acts_on(1, y, r, 2, to_y)
        e_to_x.start()
        e_to_sib.start()
        e_to_y.start()
        keep_acts().start()
        for p in range(PIECES):
            keep_grads(p).start()
        for p in range(WHOLE):
            to_the_end(opposite, p)
        to_the_middle(0)
        to_the_middle(1)
        own_out(3)
        acts_arrived(1, y, across)
        x_to_sib(1).start()
        acts_arrived(1, other_y, r)
        diagonal(1).start()
        y_to_sib(1).start()
        own_to_y().start()
        acts_arrived(0, y, across)
        x_to_sib(0).start()
        for p in range(2):
            to_the_end(far, p)
        to_the_middle(2)
        to_the_middle(3)
        own_out(4)
        for p in range(2, WHOLE):
            to_the_end(far, p)
        to_the_middle(4)
        own_out(5)
        acts_arrived(1, other_y, across)
        diagonal_to_sib(1).start()
        acts_arrived(0, other_y, r)
        diagonal(0).start()
        y_to_sib(0).start()
        to_the_middle(5)
        for p in range(PIECES):
            keep_grads(p).wait()
        sib_arrived(1)
        sum_for_end(WHOLE)
        acts_arrived(0, other_y, across)
        diagonal_to_sib(0).start()
        keep_acts().wait()
        sib_arrived(0)
        for p in range(WHOLE + 1, PIECES):
            own_product(2 * (p - WHOLE) - 2)
            own_product(2 * (p - WHOLE) - 1)
            sum_for_end(p)
        for p in range(2 * (PIECES - WHOLE) - 2, PIECES):
            own_product(p)

        e_to_x.wait_send()
        e_to_sib.wait_send()
        e_to_y.wait_send()
        x_to_sib(1).wait_send()
        diagonal(1).wait_send()
        y_to_sib(1).wait_send()
        diagonal_to_sib(1).wait_send()

        @pl.loop(0, PIECES)
        def _(p):
            own_mid(p).wait_send()
            on_mid(other_y, z, p).wait_send()
            for yy in range(2):
                on_mid(yy, mate, p).wait_send()

            @pl.when(p < WHOLE)
            def _():
                own_mate(p).wait_send()
                on_mate(other_y, z, p).wait_send()
                for zz in (opposite, far):
                    for yy in range(2):
                        on_mate(yy, zz, p).wait_send()

        for q in range(PIECES - WHOLE):
            send_sum(q).wait_send()

    own_to_x().wait_send()
    own_to_sib().wait_send()
    own_to_y().wait_send()
    x_to_sib(0).wait_send()
    diagonal(0).wait_send()
    y_to_sib(0).wait_send()
    diagonal_to_sib(0).wait_send()

    @pl.loop(0, PIECES)
    def _(p):
        swap(p).wait_send()
        write(p).wait()


def fused_body(activations, out_grads):
    width, tokens = activations.shape
    half = out_grads.shape[1] // 2
    wide = half // PIECES
    dma = pltpu.SemaphoreType.DMA
    return pl.pallas_call(
        kernel,
        out_shape=jax.ShapeDtypeStruct((width, half), jnp.float32),
        in_specs=[pl.BlockSpec(memory_space=pl.ANY)] * 2,
        out_specs=pl.BlockSpec(memory_space=pl.ANY),
        scratch_shapes=[
            pltpu.VMEM((2, 2, 4, width, tokens), jnp.bfloat16),
            pltpu.VMEM((2, 4, PIECES, tokens, wide), jnp.bfloat16),
            pltpu.VMEM((PIECES, width, wide), jnp.float32),
            pltpu.VMEM((PIECES - WHOLE, width, wide), jnp.float32),
            dma((PIECES + 1,)),
            dma((2, 2, 4)),
            dma((2, 8)),
            dma((2, 4, PIECES)),
            dma((2, 4, PIECES)),
            dma((2, 4, PIECES)),
            dma((PIECES,)),
            dma((PIECES - WHOLE,)),
            dma((PIECES - WHOLE,)),
            dma((PIECES,)),
        ],
        compiler_params=pltpu.CompilerParams(
            collective_id=0, has_side_effects=True, vmem_limit_bytes=58 * 2**20
        ),
        cost_estimate=pl.CostEstimate(
            flops=2 * half * width * tokens * 8,
            bytes_accessed=4 * half * width + 4 * tokens * (width + 2 * half),
            transcendentals=0,
        ),
    )(activations, out_grads)


def solution(mesh):
    in_specs = (P(("depth", "row"), "col"), P(("depth", "col"), "row"))
    out_specs = P(("row", "depth"), "col")
    rows, cols, depth = mesh.shape["row"], mesh.shape["col"], mesh.shape["depth"]

    def local(activations, out_grads):
        tokens, half = out_grads.shape[0], out_grads.shape[1] // depth
        fits = (rows, cols, depth) == (4, 4, 2) and half % (128 * PIECES) == 0 and tokens % 128 == 0
        if fits:
            return fused_body(activations.T, out_grads).T
        return body(activations, out_grads)

    return jax.shard_map(local, mesh=mesh, in_specs=in_specs, out_specs=out_specs, check_vma=False)
```

```python
import jax
import jax.numpy as jnp
from jax import lax
from jax.experimental import pallas as pl
from jax.experimental.pallas import tpu as pltpu
from jax.sharding import PartitionSpec as P

MESH = pl.DeviceIdType.MESH
PIECES = 6
WHOLE = 2
HALVES = 2


def contract(left, right):
    return lax.dot_general(
        left, right, (((0,), (0,)), ((), ())), preferred_element_type=jnp.float32
    )


def gather_acts(activations):
    return lax.all_gather(activations, "row", axis=0, tiled=True)


def body(activations, out_grads):
    whole_acts = gather_acts(activations)
    partial_tile = contract(lax.all_gather(out_grads, "col", axis=0, tiled=True), whole_acts)
    return lax.psum_scatter(partial_tile, "depth", scatter_dimension=0, tiled=True)


def kernel(
    acts_hbm, grads_hbm, out_hbm, acts, grads, total, sums,
    local_sem, acts_recv, acts_send, grads_recv, send_mate, send_mid, send_y,
    sums_recv, sums_send, out_sem,
):
    r, z, y = lax.axis_index("row"), lax.axis_index("col"), lax.axis_index("depth")
    wide = total.shape[2]
    half = wide * PIECES
    other_y = 1 - y
    sib = r + 1 - 2 * lax.rem(r, 2)
    across = lax.rem(r + 2, 4)
    across_sib = sib + across - r
    mate = z + 1 - 2 * lax.rem(z, 2)
    opposite = 3 - z
    far = 3 - mate
    helper = (z == 1) | (z == 2)
    to_sib, to_x, to_y, to_mate, to_mid = (
        {"row": sib}, {"row": across}, {"depth": other_y}, {"col": mate}, {"col": opposite}
    )

    barrier = pltpu.get_barrier_semaphore()
    for partner in (to_sib, to_x, to_y, to_mate):
        pl.semaphore_signal(barrier, inc=1, device_id=partner, device_id_type=MESH)

    @pl.when(helper)
    def _():
        pl.semaphore_signal(barrier, inc=1, device_id=to_mid, device_id_type=MESH)

    pl.semaphore_wait(barrier, 4 + helper.astype(jnp.int32))

    def remote(src, dst, send, recv, device):
        return pltpu.make_async_remote_copy(
            src_ref=src, dst_ref=dst, send_sem=send, recv_sem=recv,
            device_id=device, device_id_type=MESH,
        )

    def part(yy, p):
        return pl.ds(pl.multiple_of(yy * half + p * wide, wide), wide)

    def swap(p):
        return remote(
            grads_hbm.at[:, part(other_y, p)], grads.at[y, z, p],
            send_y.at[p], grads_recv.at[y, z, p], to_y,
        )

    def own_mate(p):
        return remote(
            grads_hbm.at[:, part(y, p)], grads.at[y, z, p],
            send_mate.at[y, z, p], grads_recv.at[y, z, p], to_mate,
        )

    def own_mid(p):
        return remote(
            grads_hbm.at[:, part(y, p)], grads.at[y, z, p],
            send_mid.at[y, z, p], grads_recv.at[y, z, p], to_mid,
        )

    def on_mate(yy, zz, p):
        block = grads.at[yy, zz, p]
        return remote(block, block, send_mate.at[yy, zz, p], grads_recv.at[yy, zz, p], to_mate)

    def on_mid(yy, zz, p):
        block = grads.at[yy, zz, p]
        return remote(block, block, send_mid.at[yy, zz, p], grads_recv.at[yy, zz, p], to_mid)

    def arrived(yy, zz, p):
        block = grads.at[yy, zz, p]
        pltpu.make_async_copy(block, block, grads_recv.at[yy, zz, p]).wait()

    def tokens(h):
        return pl.ds(h * (acts.shape[4] // HALVES), acts.shape[4] // HALVES)

    class Halves:
        def __init__(self, src, of, yy, rr, which, device):
            self.copy = lambda h: remote(
                src.at[:, tokens(h)], acts.at[of, yy, rr, :, tokens(h)],
                acts_send.at[of, which, h], acts_recv.at[of, yy, rr, h], device,
            )

        def start(self, halves=range(HALVES)):
            for h in halves:
                self.copy(h).start()

        def wait_send(self):
            for h in range(HALVES):
                self.copy(h).wait_send()

    def acts_on(of, yy, rr, which, device):
        return Halves(acts.at[of, yy, rr], of, yy, rr, which, device)

    def acts_arrived(of, yy, rr, halves=range(HALVES)):
        for h in halves:
            block = acts.at[of, yy, rr, :, tokens(h)]
            pltpu.make_async_copy(block, block, acts_recv.at[of, yy, rr, h]).wait()

    def own_to_x():
        return Halves(acts_hbm, 0, y, r, 0, to_x)

    def own_to_sib():
        return Halves(acts_hbm, 0, y, r, 1, to_sib)

    def own_to_y():
        return Halves(acts_hbm, 0, y, r, 2, to_y)

    def own_to_helper():
        return Halves(acts_hbm, 1, y, r, 7, to_mate)

    def x_to_sib(of):
        return acts_on(of, y, across, 3, to_sib)

    def diagonal(of):
        return acts_on(of, other_y, r, 4, to_x)

    def y_to_sib(of):
        return acts_on(of, other_y, r, 5, to_sib)

    def diagonal_to_sib(of):
        return acts_on(of, other_y, across, 6, to_sib)

    def sib_arrived(of):
        for yy in (y, other_y):
            for rr in (sib, across_sib):
                acts_arrived(of, yy, rr)

    def keep_acts():
        return pltpu.make_async_copy(acts_hbm, acts.at[0, y, r], local_sem.at[PIECES])

    def keep_grads(p):
        return pltpu.make_async_copy(grads_hbm.at[:, part(y, p)], grads.at[y, z, p], local_sem.at[p])

    def product(of, yy, zz, p):
        return jnp.dot(acts[of, yy, zz], grads[yy, zz, p], preferred_element_type=jnp.float32)

    def write(p):
        return pltpu.make_async_copy(
            total.at[p], out_hbm.at[:, pl.ds(pl.multiple_of(p * wide, wide), wide)], out_sem.at[p]
        )

    def send_sum(q):
        return remote(sums.at[q], sums.at[q], sums_send.at[q], sums_recv.at[q], to_mate)

    @pl.when(~helper)
    def _():
        own_to_helper().start()

    for p in range(PIECES // 2):
        swap(p).start()
    own_to_sib().start()

    @pl.when(~helper)
    def _():
        for p in range(PIECES // 2, PIECES):
            swap(p).start()
        own_to_x().start()
        for p in range(PIECES):
            own_mate(p).start()
            arrived(other_y, z, p)
            on_mate(other_y, z, p).start()
        own_to_y().start()
        keep_acts().start()
        for p in range(PIECES):
            keep_grads(p).start()
        acts_arrived(0, y, across)
        x_to_sib(0).start()
        acts_arrived(0, other_y, r)
        diagonal(0).start()
        y_to_sib(0).start()
        acts_arrived(0, other_y, across)
        diagonal_to_sib(0).start()
        keep_acts().wait()
        for p in range(PIECES):
            keep_grads(p).wait()
        sib_arrived(0)

        @pl.loop(0, PIECES)
        def _(p):
            total[p] = product(0, 0, z, p)
            total[p] += product(0, 1, z, p)

        for zz in (mate, far, opposite):
            @pl.loop(0, WHOLE * 2)
            def _(i):
                p, yy = i // 2, lax.rem(y + i, 2)
                arrived(yy, zz, p)
                total[p] += product(0, yy, zz, p)

        for p in range(WHOLE):
            write(p).start()

        @pl.loop(WHOLE, PIECES)
        def _(p):
            q = p - WHOLE
            pltpu.make_async_copy(sums.at[q], sums.at[q], sums_recv.at[q]).wait()
            total[p] += sums[q]
            write(p).start()

        own_to_helper().wait_send()

        @pl.loop(0, PIECES)
        def _(p):
            own_mate(p).wait_send()
            on_mate(other_y, z, p).wait_send()

    @pl.when(helper)
    def _():
        def own_out(p):
            own_mid(p).start()
            if p < WHOLE:
                own_mate(p).start()
            arrived(other_y, z, p)
            on_mid(other_y, z, p).start()
            if p < WHOLE:
                on_mate(other_y, z, p).start()

        def to_the_end(zz, p):
            for yy in (y, other_y):
                arrived(yy, zz, p)
                if p < WHOLE:
                    on_mate(yy, zz, p).start()

        def to_the_middle(p):
            for yy in (y, other_y):
                arrived(yy, mate, p)
                on_mid(yy, mate, p).start()

        def own_product(p):
            total[p] = product(0, 0, 0, p)

            @pl.loop(1, 8)
            def _(i):
                total[p] += product(0, i // 4, lax.rem(i, 4), p)

            write(p).start()

        def sum_for_end(p):
            q = p - WHOLE
            to_the_end(opposite, p)
            sums[q] = product(1, 0, z, p)
            sums[q] += product(1, 1, z, p)

            @pl.loop(0, 2)
            def _(yy):
                sums[q] += product(1, yy, opposite, p)

            to_the_end(far, p)

            @pl.loop(0, 2)
            def _(yy):
                sums[q] += product(1, yy, far, p)

            send_sum(q).start()

        e_to_x = acts_on(1, y, r, 0, to_x)
        e_to_sib = acts_on(1, y, r, 1, to_sib)
        e_to_y = acts_on(1, y, r, 2, to_y)
        own_out(0)
        own_out(1)
        for h in range(HALVES):
            acts_arrived(1, y, r, (h,))
            e_to_x.start((h,))
            e_to_y.start((h,))
            e_to_sib.start((h,))
            if h == 0:
                own_out(2)
        for p in range(PIECES // 2, PIECES):
            swap(p).start()
        keep_acts().start()
        for p in range(PIECES):
            keep_grads(p).start()
        for p in range(WHOLE):
            to_the_end(opposite, p)
        for h in range(HALVES):
            acts_arrived(1, y, across, (h,))
            x_to_sib(1).start((h,))
            acts_arrived(1, other_y, r, (h,))
            diagonal(1).start((h,))
            y_to_sib(1).start((h,))
            to_the_middle(h)
        own_to_x().start()
        own_to_y().start()
        to_the_end(far, 0)
        to_the_middle(2)
        own_out(3)
        to_the_end(far, 1)
        acts_arrived(1, other_y, across)
        diagonal_to_sib(1).start()
        to_the_middle(3)
        own_out(4)
        for p in range(PIECES):
            keep_grads(p).wait()
        sib_arrived(1)
        sum_for_end(2)
        to_the_middle(4)
        own_out(5)
        acts_arrived(0, other_y, r)
        diagonal(0).start()
        y_to_sib(0).start()
        acts_arrived(0, y, across)
        x_to_sib(0).start()
        to_the_middle(5)
        sum_for_end(3)
        acts_arrived(0, other_y, across)
        diagonal_to_sib(0).start()
        keep_acts().wait()
        sib_arrived(0)
        own_product(0)
        own_product(1)
        sum_for_end(4)
        for p in range(2, 5):
            own_product(p)
        sum_for_end(5)
        own_product(5)

        e_to_x.wait_send()
        e_to_sib.wait_send()
        e_to_y.wait_send()
        x_to_sib(1).wait_send()
        diagonal(1).wait_send()
        y_to_sib(1).wait_send()
        diagonal_to_sib(1).wait_send()

        @pl.loop(0, PIECES)
        def _(p):
            own_mid(p).wait_send()
            on_mid(other_y, z, p).wait_send()
            for yy in range(2):
                on_mid(yy, mate, p).wait_send()

            @pl.when(p < WHOLE)
            def _():
                own_mate(p).wait_send()
                on_mate(other_y, z, p).wait_send()
                for zz in (opposite, far):
                    for yy in range(2):
                        on_mate(yy, zz, p).wait_send()

        for q in range(PIECES - WHOLE):
            send_sum(q).wait_send()

    own_to_x().wait_send()
    own_to_sib().wait_send()
    own_to_y().wait_send()
    x_to_sib(0).wait_send()
    diagonal(0).wait_send()
    y_to_sib(0).wait_send()
    diagonal_to_sib(0).wait_send()

    @pl.loop(0, PIECES)
    def _(p):
        swap(p).wait_send()
        write(p).wait()


def fused_body(activations, out_grads):
    width, tokens = activations.shape
    half = out_grads.shape[1] // 2
    wide = half // PIECES
    dma = pltpu.SemaphoreType.DMA
    return pl.pallas_call(
        kernel,
        out_shape=pltpu.VMEM((width, half), jnp.float32),
        in_specs=[pl.BlockSpec(memory_space=pltpu.HBM)] * 2,
        out_specs=pl.BlockSpec(memory_space=pl.ANY),
        scratch_shapes=[
            pltpu.VMEM((2, 2, 4, width, tokens), jnp.bfloat16),
            pltpu.VMEM((2, 4, PIECES, tokens, wide), jnp.bfloat16),
            pltpu.VMEM((PIECES, width, wide), jnp.float32),
            pltpu.VMEM((PIECES - WHOLE, width, wide), jnp.float32),
            dma((PIECES + 1,)),
            dma((2, 2, 4, HALVES)),
            dma((2, 8, HALVES)),
            dma((2, 4, PIECES)),
            dma((2, 4, PIECES)),
            dma((2, 4, PIECES)),
            dma((PIECES,)),
            dma((PIECES - WHOLE,)),
            dma((PIECES - WHOLE,)),
            dma((PIECES,)),
        ],
        compiler_params=pltpu.CompilerParams(
            collective_id=0, has_side_effects=True, vmem_limit_bytes=44 * 2**20
        ),
        cost_estimate=pl.CostEstimate(
            flops=2 * half * width * tokens * 8,
            bytes_accessed=4 * half * width + 4 * tokens * (width + 2 * half),
            transcendentals=0,
        ),
    )(*(pltpu.with_memory_space_constraint(x, pltpu.HBM) for x in (activations, out_grads)))


def solution(mesh):
    in_specs = (P(("depth", "row"), "col"), P(("depth", "col"), "row"))
    out_specs = P(("row", "depth"), "col")
    rows, cols, depth = mesh.shape["row"], mesh.shape["col"], mesh.shape["depth"]

    def local(activations, out_grads):
        tokens, half = out_grads.shape[0], out_grads.shape[1] // depth
        fits = (rows, cols, depth) == (4, 4, 2) and half % (128 * PIECES) == 0 and tokens % (128 * HALVES) == 0
        if fits:
            return fused_body(activations.T, out_grads).T
        return body(activations, out_grads)

    return jax.shard_map(local, mesh=mesh, in_specs=in_specs, out_specs=out_specs, check_vma=False)
```

```python
import jax
import jax.numpy as jnp
from jax import lax
from jax.experimental import pallas as pl
from jax.experimental.pallas import tpu as pltpu
from jax.sharding import PartitionSpec as P

MESH = pl.DeviceIdType.MESH
PIECES = 6
WHOLE = 2
HALVES = 2


def contract(left, right):
    return lax.dot_general(
        left, right, (((0,), (0,)), ((), ())), preferred_element_type=jnp.float32
    )


def gather_acts(activations):
    return lax.all_gather(activations, "row", axis=0, tiled=True)


def body(activations, out_grads):
    whole_acts = gather_acts(activations)
    partial_tile = contract(lax.all_gather(out_grads, "col", axis=0, tiled=True), whole_acts)
    return lax.psum_scatter(partial_tile, "depth", scatter_dimension=0, tiled=True)


def kernel(
    acts_hbm, grads_hbm, out_hbm, acts, grads, total, sums,
    local_sem, acts_recv, acts_send, grads_recv, send_mate, send_mid, send_y,
    sums_recv, sums_send, out_sem,
):
    r, z, y = lax.axis_index("row"), lax.axis_index("col"), lax.axis_index("depth")
    wide = total.shape[2]
    half = wide * PIECES
    other_y = 1 - y
    sib = r + 1 - 2 * lax.rem(r, 2)
    across = lax.rem(r + 2, 4)
    across_sib = sib + across - r
    mate = z + 1 - 2 * lax.rem(z, 2)
    opposite = 3 - z
    far = 3 - mate
    helper = (z == 1) | (z == 2)
    to_sib, to_x, to_y, to_mate, to_mid = (
        {"row": sib}, {"row": across}, {"depth": other_y}, {"col": mate}, {"col": opposite}
    )

    barrier = pltpu.get_barrier_semaphore()
    for partner in (to_sib, to_x, to_y, to_mate):
        pl.semaphore_signal(barrier, inc=1, device_id=partner, device_id_type=MESH)

    @pl.when(helper)
    def _():
        pl.semaphore_signal(barrier, inc=1, device_id=to_mid, device_id_type=MESH)

    pl.semaphore_wait(barrier, 4 + helper.astype(jnp.int32))

    def remote(src, dst, send, recv, device):
        return pltpu.make_async_remote_copy(
            src_ref=src, dst_ref=dst, send_sem=send, recv_sem=recv,
            device_id=device, device_id_type=MESH,
        )

    def part(yy, p):
        return pl.ds(pl.multiple_of(yy * half + p * wide, wide), wide)

    def swap(p):
        return remote(
            grads_hbm.at[:, part(other_y, p)], grads.at[y, z, p],
            send_y.at[p], grads_recv.at[y, z, p], to_y,
        )

    def own_mate(p):
        return remote(
            grads_hbm.at[:, part(y, p)], grads.at[y, z, p],
            send_mate.at[y, z, p], grads_recv.at[y, z, p], to_mate,
        )

    def own_mid(p):
        return remote(
            grads_hbm.at[:, part(y, p)], grads.at[y, z, p],
            send_mid.at[y, z, p], grads_recv.at[y, z, p], to_mid,
        )

    def on_mate(yy, zz, p):
        block = grads.at[yy, zz, p]
        return remote(block, block, send_mate.at[yy, zz, p], grads_recv.at[yy, zz, p], to_mate)

    def on_mid(yy, zz, p):
        block = grads.at[yy, zz, p]
        return remote(block, block, send_mid.at[yy, zz, p], grads_recv.at[yy, zz, p], to_mid)

    def arrived(yy, zz, p):
        block = grads.at[yy, zz, p]
        pltpu.make_async_copy(block, block, grads_recv.at[yy, zz, p]).wait()

    def tokens(h):
        return pl.ds(h * (acts.shape[4] // HALVES), acts.shape[4] // HALVES)

    class Halves:
        def __init__(self, src, of, yy, rr, which, device):
            self.copy = lambda h: remote(
                src.at[:, tokens(h)], acts.at[of, yy, rr, :, tokens(h)],
                acts_send.at[of, which, h], acts_recv.at[of, yy, rr, h], device,
            )

        def start(self, halves=range(HALVES)):
            for h in halves:
                self.copy(h).start()

        def wait_send(self):
            for h in range(HALVES):
                self.copy(h).wait_send()

    def acts_on(of, yy, rr, which, device):
        return Halves(acts.at[of, yy, rr], of, yy, rr, which, device)

    def acts_arrived(of, yy, rr, halves=range(HALVES)):
        for h in halves:
            block = acts.at[of, yy, rr, :, tokens(h)]
            pltpu.make_async_copy(block, block, acts_recv.at[of, yy, rr, h]).wait()

    def own_to_x():
        return Halves(acts_hbm, 0, y, r, 0, to_x)

    def own_to_sib():
        return Halves(acts_hbm, 0, y, r, 1, to_sib)

    def own_to_y():
        return Halves(acts_hbm, 0, y, r, 2, to_y)

    def own_to_helper():
        return Halves(acts_hbm, 1, y, r, 7, to_mate)

    def x_to_sib(of):
        return acts_on(of, y, across, 3, to_sib)

    def diagonal_x(of):
        return acts_on(of, other_y, r, 4, to_x).copy(0)

    def diagonal_y(of):
        return acts_on(of, y, across, 4, to_y).copy(1)

    def y_to_sib(of):
        return acts_on(of, other_y, r, 5, to_sib)

    def diagonal_to_sib(of):
        return acts_on(of, other_y, across, 6, to_sib)

    def sib_arrived(of):
        for yy in (y, other_y):
            for rr in (sib, across_sib):
                acts_arrived(of, yy, rr)

    def keep_acts():
        return pltpu.make_async_copy(acts_hbm, acts.at[0, y, r], local_sem.at[PIECES])

    def keep_grads(p):
        return pltpu.make_async_copy(grads_hbm.at[:, part(y, p)], grads.at[y, z, p], local_sem.at[p])

    def product(of, yy, zz, p):
        return jnp.dot(acts[of, yy, zz], grads[yy, zz, p], preferred_element_type=jnp.float32)

    def write(p):
        return pltpu.make_async_copy(
            total.at[p], out_hbm.at[:, pl.ds(pl.multiple_of(p * wide, wide), wide)], out_sem.at[p]
        )

    def send_sum(q):
        return remote(sums.at[q], sums.at[q], sums_send.at[q], sums_recv.at[q], to_mate)

    @pl.when(~helper)
    def _():
        own_to_helper().start()

    for p in range(PIECES // 2):
        swap(p).start()
    own_to_sib().start()

    @pl.when(~helper)
    def _():
        for p in range(PIECES // 2, PIECES):
            swap(p).start()
        own_to_x().start()
        for p in range(PIECES):
            own_mate(p).start()
            arrived(other_y, z, p)
            on_mate(other_y, z, p).start()
        own_to_y().start()
        keep_acts().start()
        for p in range(PIECES):
            keep_grads(p).start()
        acts_arrived(0, y, across)
        x_to_sib(0).start()
        diagonal_y(0).start()
        acts_arrived(0, other_y, r)
        diagonal_x(0).start()
        y_to_sib(0).start()
        acts_arrived(0, other_y, across)
        diagonal_to_sib(0).start()
        keep_acts().wait()
        for p in range(PIECES):
            keep_grads(p).wait()
        sib_arrived(0)

        @pl.loop(0, PIECES)
        def _(p):
            total[p] = product(0, 0, z, p)
            total[p] += product(0, 1, z, p)

        for zz in (mate, far, opposite):
            @pl.loop(0, WHOLE * 2)
            def _(i):
                p, yy = i // 2, lax.rem(y + i, 2)
                arrived(yy, zz, p)
                total[p] += product(0, yy, zz, p)

        for p in range(WHOLE):
            write(p).start()

        @pl.loop(WHOLE, PIECES)
        def _(p):
            q = p - WHOLE
            pltpu.make_async_copy(sums.at[q], sums.at[q], sums_recv.at[q]).wait()
            total[p] += sums[q]
            write(p).start()

        own_to_helper().wait_send()

        @pl.loop(0, PIECES)
        def _(p):
            own_mate(p).wait_send()
            on_mate(other_y, z, p).wait_send()

    @pl.when(helper)
    def _():
        def own_out(p):
            own_mid(p).start()
            if p < WHOLE:
                own_mate(p).start()
            arrived(other_y, z, p)
            on_mid(other_y, z, p).start()
            if p < WHOLE:
                on_mate(other_y, z, p).start()

        def to_the_end(zz, p):
            for yy in (y, other_y):
                arrived(yy, zz, p)
                if p < WHOLE:
                    on_mate(yy, zz, p).start()

        def to_the_middle(p):
            for yy in (y, other_y):
                arrived(yy, mate, p)
                on_mid(yy, mate, p).start()

        def own_product(p):
            total[p] = product(0, 0, 0, p)

            @pl.loop(1, 8)
            def _(i):
                total[p] += product(0, i // 4, lax.rem(i, 4), p)

            write(p).start()

        def sum_for_end(p):
            q = p - WHOLE
            to_the_end(opposite, p)
            sums[q] = product(1, 0, z, p)
            sums[q] += product(1, 1, z, p)

            @pl.loop(0, 2)
            def _(yy):
                sums[q] += product(1, yy, opposite, p)

            to_the_end(far, p)

            @pl.loop(0, 2)
            def _(yy):
                sums[q] += product(1, yy, far, p)

            send_sum(q).start()

        e_to_x = acts_on(1, y, r, 0, to_x)
        e_to_sib = acts_on(1, y, r, 1, to_sib)
        e_to_y = acts_on(1, y, r, 2, to_y)
        own_out(0)
        own_out(1)
        for h in range(HALVES):
            acts_arrived(1, y, r, (h,))
            e_to_x.start((h,))
            e_to_y.start((h,))
            e_to_sib.start((h,))
            if h == 0:
                own_out(2)
        keep_acts().start()
        for p in range(PIECES):
            keep_grads(p).start()
        for p in range(WHOLE):
            to_the_end(opposite, p)
        acts_arrived(1, y, across, (0,))
        x_to_sib(1).start((0,))
        acts_arrived(1, other_y, r, (0,))
        diagonal_x(1).start()
        y_to_sib(1).start((0,))
        to_the_middle(0)
        acts_arrived(1, y, across, (1,))
        diagonal_y(1).start()
        x_to_sib(1).start((1,))
        acts_arrived(1, other_y, r, (1,))
        y_to_sib(1).start((1,))
        for p in range(PIECES // 2, PIECES):
            swap(p).start()
        own_to_x().start()
        own_to_y().start()
        to_the_end(far, 0)
        to_the_middle(1)
        for h in range(HALVES):
            acts_arrived(1, other_y, across, (h,))
            diagonal_to_sib(1).start((h,))
        to_the_end(far, 1)
        to_the_middle(2)
        own_out(3)
        for p in range(PIECES):
            keep_grads(p).wait()
        sib_arrived(1)
        sum_for_end(2)
        to_the_middle(3)
        own_out(4)
        to_the_middle(4)
        sum_for_end(3)
        own_out(5)
        to_the_middle(5)
        acts_arrived(0, y, across)
        diagonal_y(0).start()
        x_to_sib(0).start()
        acts_arrived(0, other_y, r)
        diagonal_x(0).start()
        y_to_sib(0).start()
        acts_arrived(0, other_y, across)
        diagonal_to_sib(0).start()
        keep_acts().wait()
        sib_arrived(0)
        sum_for_end(4)
        for p in range(5):
            own_product(p)
        sum_for_end(5)
        own_product(5)

        e_to_x.wait_send()
        e_to_sib.wait_send()
        e_to_y.wait_send()
        x_to_sib(1).wait_send()
        diagonal_x(1).wait_send()
        diagonal_y(1).wait_send()
        y_to_sib(1).wait_send()
        diagonal_to_sib(1).wait_send()

        @pl.loop(0, PIECES)
        def _(p):
            own_mid(p).wait_send()
            on_mid(other_y, z, p).wait_send()
            for yy in range(2):
                on_mid(yy, mate, p).wait_send()

            @pl.when(p < WHOLE)
            def _():
                own_mate(p).wait_send()
                on_mate(other_y, z, p).wait_send()
                for zz in (opposite, far):
                    for yy in range(2):
                        on_mate(yy, zz, p).wait_send()

        for q in range(PIECES - WHOLE):
            send_sum(q).wait_send()

    own_to_x().wait_send()
    own_to_sib().wait_send()
    own_to_y().wait_send()
    x_to_sib(0).wait_send()
    diagonal_x(0).wait_send()
    diagonal_y(0).wait_send()
    y_to_sib(0).wait_send()
    diagonal_to_sib(0).wait_send()

    @pl.loop(0, PIECES)
    def _(p):
        swap(p).wait_send()
        write(p).wait()


def fused_body(activations, out_grads):
    width, tokens = activations.shape
    half = out_grads.shape[1] // 2
    wide = half // PIECES
    dma = pltpu.SemaphoreType.DMA
    return pl.pallas_call(
        kernel,
        out_shape=pltpu.VMEM((width, half), jnp.float32),
        in_specs=[pl.BlockSpec(memory_space=pltpu.HBM)] * 2,
        out_specs=pl.BlockSpec(memory_space=pl.ANY),
        scratch_shapes=[
            pltpu.VMEM((2, 2, 4, width, tokens), jnp.bfloat16),
            pltpu.VMEM((2, 4, PIECES, tokens, wide), jnp.bfloat16),
            pltpu.VMEM((PIECES, width, wide), jnp.float32),
            pltpu.VMEM((PIECES - WHOLE, width, wide), jnp.float32),
            dma((PIECES + 1,)),
            dma((2, 2, 4, HALVES)),
            dma((2, 8, HALVES)),
            dma((2, 4, PIECES)),
            dma((2, 4, PIECES)),
            dma((2, 4, PIECES)),
            dma((PIECES,)),
            dma((PIECES - WHOLE,)),
            dma((PIECES - WHOLE,)),
            dma((PIECES,)),
        ],
        compiler_params=pltpu.CompilerParams(
            collective_id=0, has_side_effects=True, vmem_limit_bytes=44 * 2**20
        ),
        cost_estimate=pl.CostEstimate(
            flops=2 * half * width * tokens * 8,
            bytes_accessed=4 * half * width + 4 * tokens * (width + 2 * half),
            transcendentals=0,
        ),
    )(*(pltpu.with_memory_space_constraint(x, pltpu.HBM) for x in (activations, out_grads)))


def solution(mesh):
    in_specs = (P(("depth", "row"), "col"), P(("depth", "col"), "row"))
    out_specs = P(("row", "depth"), "col")
    rows, cols, depth = mesh.shape["row"], mesh.shape["col"], mesh.shape["depth"]

    def local(activations, out_grads):
        tokens, half = out_grads.shape[0], out_grads.shape[1] // depth
        fits = (rows, cols, depth) == (4, 4, 2) and half % (128 * PIECES) == 0 and tokens % (128 * HALVES) == 0
        if fits:
            return fused_body(activations.T, out_grads).T
        return body(activations, out_grads)

    return jax.shard_map(local, mesh=mesh, in_specs=in_specs, out_specs=out_specs, check_vma=False)
```

```python
import jax
import jax.numpy as jnp
from jax import lax
from jax.experimental import pallas as pl
from jax.experimental.pallas import tpu as pltpu
from jax.sharding import PartitionSpec as P

MESH = pl.DeviceIdType.MESH
PIECES = 6
WHOLE = 2
HALVES = 2


def contract(left, right):
    return lax.dot_general(
        left, right, (((0,), (0,)), ((), ())), preferred_element_type=jnp.float32
    )


def gather_acts(activations):
    return lax.all_gather(activations, "row", axis=0, tiled=True)


def body(activations, out_grads):
    whole_acts = gather_acts(activations)
    partial_tile = contract(lax.all_gather(out_grads, "col", axis=0, tiled=True), whole_acts)
    return lax.psum_scatter(partial_tile, "depth", scatter_dimension=0, tiled=True)


def kernel(
    acts_hbm, grads_hbm, out_ref, acts, grads, sums,
    local_sem, acts_recv, acts_send, grads_recv, send_mate, send_mid, send_y,
    sums_recv, sums_send,
):
    r, z, y = lax.axis_index("row"), lax.axis_index("col"), lax.axis_index("depth")
    wide = sums.shape[2]
    half = wide * PIECES
    other_y = 1 - y
    sib = r + 1 - 2 * lax.rem(r, 2)
    across = lax.rem(r + 2, 4)
    across_sib = sib + across - r
    mate = z + 1 - 2 * lax.rem(z, 2)
    opposite = 3 - z
    far = 3 - mate
    helper = (z == 1) | (z == 2)
    to_sib, to_x, to_y, to_mate, to_mid = (
        {"row": sib}, {"row": across}, {"depth": other_y}, {"col": mate}, {"col": opposite}
    )

    barrier = pltpu.get_barrier_semaphore()
    for partner in (to_sib, to_x, to_y, to_mate):
        pl.semaphore_signal(barrier, inc=1, device_id=partner, device_id_type=MESH)

    @pl.when(helper)
    def _():
        pl.semaphore_signal(barrier, inc=1, device_id=to_mid, device_id_type=MESH)

    pl.semaphore_wait(barrier, 4 + helper.astype(jnp.int32))

    def remote(src, dst, send, recv, device):
        return pltpu.make_async_remote_copy(
            src_ref=src, dst_ref=dst, send_sem=send, recv_sem=recv,
            device_id=device, device_id_type=MESH,
        )

    def part(yy, p):
        return pl.ds(pl.multiple_of(yy * half + p * wide, wide), wide)

    def swap(p):
        return remote(
            grads_hbm.at[:, part(other_y, p)], grads.at[y, z, p],
            send_y.at[p], grads_recv.at[y, z, p], to_y,
        )

    def own_mate(p):
        return remote(
            grads_hbm.at[:, part(y, p)], grads.at[y, z, p],
            send_mate.at[y, z, p], grads_recv.at[y, z, p], to_mate,
        )

    def own_mid(p):
        return remote(
            grads_hbm.at[:, part(y, p)], grads.at[y, z, p],
            send_mid.at[y, z, p], grads_recv.at[y, z, p], to_mid,
        )

    def on_mate(yy, zz, p):
        block = grads.at[yy, zz, p]
        return remote(block, block, send_mate.at[yy, zz, p], grads_recv.at[yy, zz, p], to_mate)

    def on_mid(yy, zz, p):
        block = grads.at[yy, zz, p]
        return remote(block, block, send_mid.at[yy, zz, p], grads_recv.at[yy, zz, p], to_mid)

    def arrived(yy, zz, p):
        block = grads.at[yy, zz, p]
        pltpu.make_async_copy(block, block, grads_recv.at[yy, zz, p]).wait()

    def tokens(h):
        return pl.ds(h * (acts.shape[4] // HALVES), acts.shape[4] // HALVES)

    class Halves:
        def __init__(self, src, of, yy, rr, which, device):
            self.copy = lambda h: remote(
                src.at[:, tokens(h)], acts.at[of, yy, rr, :, tokens(h)],
                acts_send.at[of, which, h], acts_recv.at[of, yy, rr, h], device,
            )

        def start(self, halves=range(HALVES)):
            for h in halves:
                self.copy(h).start()

        def wait_send(self):
            for h in range(HALVES):
                self.copy(h).wait_send()

    def acts_on(of, yy, rr, which, device):
        return Halves(acts.at[of, yy, rr], of, yy, rr, which, device)

    def acts_arrived(of, yy, rr, halves=range(HALVES)):
        for h in halves:
            block = acts.at[of, yy, rr, :, tokens(h)]
            pltpu.make_async_copy(block, block, acts_recv.at[of, yy, rr, h]).wait()

    def own_to_x():
        return Halves(acts_hbm, 0, y, r, 0, to_x)

    def own_to_sib():
        return Halves(acts_hbm, 0, y, r, 1, to_sib)

    def own_to_y():
        return Halves(acts_hbm, 0, y, r, 2, to_y)

    def own_to_helper():
        return Halves(acts_hbm, 1, y, r, 7, to_mate)

    def x_to_sib(of):
        return acts_on(of, y, across, 3, to_sib)

    def diagonal_x(of):
        return acts_on(of, other_y, r, 4, to_x).copy(0)

    def diagonal_y(of):
        return acts_on(of, y, across, 4, to_y).copy(1)

    def y_to_sib(of):
        return acts_on(of, other_y, r, 5, to_sib)

    def diagonal_to_sib(of):
        return acts_on(of, other_y, across, 6, to_sib)

    def sib_arrived(of):
        for yy in (y, other_y):
            for rr in (sib, across_sib):
                acts_arrived(of, yy, rr)

    def keep_acts():
        return pltpu.make_async_copy(acts_hbm, acts.at[0, y, r], local_sem.at[PIECES])

    def keep_grads(p):
        return pltpu.make_async_copy(grads_hbm.at[:, part(y, p)], grads.at[y, z, p], local_sem.at[p])

    def product(of, yy, zz, p):
        return jnp.dot(acts[of, yy, zz], grads[yy, zz, p], preferred_element_type=jnp.float32)

    def column(p):
        return pl.ds(pl.multiple_of(p * wide, wide), wide)

    def send_sum(q):
        return remote(sums.at[q], sums.at[q], sums_send.at[q], sums_recv.at[q], to_mate)

    @pl.when(~helper)
    def _():
        own_to_helper().start()

    for p in range(PIECES // 2):
        swap(p).start()
    own_to_sib().start()

    @pl.when(~helper)
    def _():
        for p in range(PIECES // 2, PIECES):
            swap(p).start()
        own_to_x().start()
        for p in range(PIECES):
            own_mate(p).start()
            arrived(other_y, z, p)
            on_mate(other_y, z, p).start()
        own_to_y().start()
        keep_acts().start()
        for p in range(PIECES):
            keep_grads(p).start()
        acts_arrived(0, y, across)
        x_to_sib(0).start()
        diagonal_y(0).start()
        acts_arrived(0, other_y, r)
        diagonal_x(0).start()
        y_to_sib(0).start()
        acts_arrived(0, other_y, across)
        diagonal_to_sib(0).start()
        keep_acts().wait()
        for p in range(PIECES):
            keep_grads(p).wait()
        sib_arrived(0)

        @pl.loop(0, PIECES)
        def _(p):
            out_ref[:, column(p)] = product(0, 0, z, p)
            out_ref[:, column(p)] += product(0, 1, z, p)

        for zz in (mate, far, opposite):
            @pl.loop(0, WHOLE * 2)
            def _(i):
                p, yy = i // 2, lax.rem(y + i, 2)
                arrived(yy, zz, p)
                out_ref[:, column(p)] += product(0, yy, zz, p)

        @pl.loop(WHOLE, PIECES)
        def _(p):
            q = p - WHOLE
            pltpu.make_async_copy(sums.at[q], sums.at[q], sums_recv.at[q]).wait()
            out_ref[:, column(p)] += sums[q]

        own_to_helper().wait_send()

        @pl.loop(0, PIECES)
        def _(p):
            own_mate(p).wait_send()
            on_mate(other_y, z, p).wait_send()

    @pl.when(helper)
    def _():
        def own_out(p):
            own_mid(p).start()
            if p < WHOLE:
                own_mate(p).start()
            arrived(other_y, z, p)
            on_mid(other_y, z, p).start()
            if p < WHOLE:
                on_mate(other_y, z, p).start()

        def to_the_end(zz, p):
            for yy in (y, other_y):
                arrived(yy, zz, p)
                if p < WHOLE:
                    on_mate(yy, zz, p).start()

        def to_the_middle(p):
            for yy in (y, other_y):
                arrived(yy, mate, p)
                on_mid(yy, mate, p).start()

        def own_product(p):
            out_ref[:, column(p)] = product(0, 0, 0, p)

            @pl.loop(1, 8)
            def _(i):
                out_ref[:, column(p)] += product(0, i // 4, lax.rem(i, 4), p)


        def sum_for_end(p):
            q = p - WHOLE
            to_the_end(opposite, p)
            sums[q] = product(1, 0, z, p)
            sums[q] += product(1, 1, z, p)

            @pl.loop(0, 2)
            def _(yy):
                sums[q] += product(1, yy, opposite, p)

            to_the_end(far, p)

            @pl.loop(0, 2)
            def _(yy):
                sums[q] += product(1, yy, far, p)

            send_sum(q).start()

        e_to_x = acts_on(1, y, r, 0, to_x)
        e_to_sib = acts_on(1, y, r, 1, to_sib)
        e_to_y = acts_on(1, y, r, 2, to_y)
        own_out(0)
        own_out(1)
        for h in range(HALVES):
            acts_arrived(1, y, r, (h,))
            e_to_x.start((h,))
            e_to_y.start((h,))
            e_to_sib.start((h,))
            if h == 0:
                own_out(2)
        keep_acts().start()
        for p in range(PIECES):
            keep_grads(p).start()
        for p in range(WHOLE):
            to_the_end(opposite, p)
        acts_arrived(1, y, across, (0,))
        x_to_sib(1).start((0,))
        acts_arrived(1, other_y, r, (0,))
        diagonal_x(1).start()
        y_to_sib(1).start((0,))
        to_the_middle(0)
        acts_arrived(1, y, across, (1,))
        diagonal_y(1).start()
        x_to_sib(1).start((1,))
        acts_arrived(1, other_y, r, (1,))
        y_to_sib(1).start((1,))
        for p in range(PIECES // 2, PIECES):
            swap(p).start()
        own_to_x().start()
        own_to_y().start()
        to_the_end(far, 0)
        to_the_middle(1)
        for h in range(HALVES):
            acts_arrived(1, other_y, across, (h,))
            diagonal_to_sib(1).start((h,))
        to_the_end(far, 1)
        to_the_middle(2)
        own_out(3)
        for p in range(PIECES):
            keep_grads(p).wait()
        sib_arrived(1)
        sum_for_end(2)
        to_the_middle(3)
        own_out(4)
        to_the_middle(4)
        sum_for_end(3)
        own_out(5)
        to_the_middle(5)
        acts_arrived(0, y, across)
        diagonal_y(0).start()
        x_to_sib(0).start()
        acts_arrived(0, other_y, r)
        diagonal_x(0).start()
        y_to_sib(0).start()
        acts_arrived(0, other_y, across)
        diagonal_to_sib(0).start()
        keep_acts().wait()
        sib_arrived(0)
        sum_for_end(4)
        for p in range(5):
            own_product(p)
        sum_for_end(5)
        own_product(5)

        e_to_x.wait_send()
        e_to_sib.wait_send()
        e_to_y.wait_send()
        x_to_sib(1).wait_send()
        diagonal_x(1).wait_send()
        diagonal_y(1).wait_send()
        y_to_sib(1).wait_send()
        diagonal_to_sib(1).wait_send()

        @pl.loop(0, PIECES)
        def _(p):
            own_mid(p).wait_send()
            on_mid(other_y, z, p).wait_send()
            for yy in range(2):
                on_mid(yy, mate, p).wait_send()

            @pl.when(p < WHOLE)
            def _():
                own_mate(p).wait_send()
                on_mate(other_y, z, p).wait_send()
                for zz in (opposite, far):
                    for yy in range(2):
                        on_mate(yy, zz, p).wait_send()

        for q in range(PIECES - WHOLE):
            send_sum(q).wait_send()

    own_to_x().wait_send()
    own_to_sib().wait_send()
    own_to_y().wait_send()
    x_to_sib(0).wait_send()
    diagonal_x(0).wait_send()
    diagonal_y(0).wait_send()
    y_to_sib(0).wait_send()
    diagonal_to_sib(0).wait_send()

    @pl.loop(0, PIECES)
    def _(p):
        swap(p).wait_send()


def fused_body(activations, out_grads):
    width, tokens = activations.shape
    half = out_grads.shape[1] // 2
    wide = half // PIECES
    dma = pltpu.SemaphoreType.DMA
    return pl.pallas_call(
        kernel,
        out_shape=pltpu.VMEM((width, half), jnp.float32),
        in_specs=[pl.BlockSpec(memory_space=pltpu.HBM)] * 2,
        out_specs=pl.BlockSpec(memory_space=pltpu.VMEM),
        scratch_shapes=[
            pltpu.VMEM((2, 2, 4, width, tokens), jnp.bfloat16),
            pltpu.VMEM((2, 4, PIECES, tokens, wide), jnp.bfloat16),
            pltpu.VMEM((PIECES - WHOLE, width, wide), jnp.float32),
            dma((PIECES + 1,)),
            dma((2, 2, 4, HALVES)),
            dma((2, 8, HALVES)),
            dma((2, 4, PIECES)),
            dma((2, 4, PIECES)),
            dma((2, 4, PIECES)),
            dma((PIECES,)),
            dma((PIECES - WHOLE,)),
            dma((PIECES - WHOLE,)),
        ],
        compiler_params=pltpu.CompilerParams(
            collective_id=0, has_side_effects=True, vmem_limit_bytes=44 * 2**20
        ),
        cost_estimate=pl.CostEstimate(
            flops=2 * half * width * tokens * 8,
            bytes_accessed=4 * half * width + 4 * tokens * (width + 2 * half),
            transcendentals=0,
        ),
    )(*(pltpu.with_memory_space_constraint(x, pltpu.HBM) for x in (activations, out_grads)))


def solution(mesh):
    in_specs = (P(("depth", "row"), "col"), P(("depth", "col"), "row"))
    out_specs = P(("row", "depth"), "col")
    rows, cols, depth = mesh.shape["row"], mesh.shape["col"], mesh.shape["depth"]

    def local(activations, out_grads):
        tokens, half = out_grads.shape[0], out_grads.shape[1] // depth
        fits = (rows, cols, depth) == (4, 4, 2) and half % (128 * PIECES) == 0 and tokens % (128 * HALVES) == 0
        if fits:
            return fused_body(activations.T, out_grads).T
        return body(activations, out_grads)

    return jax.shard_map(local, mesh=mesh, in_specs=in_specs, out_specs=out_specs, check_vma=False)
```
